256 devices in a mesh: qr: 16 (over y, x), pc: 16 (over z, core).
Axes of the slice: x: 4, y: 4, z: 8, core: 2. Of those that a mesh axis runs over, the one named last changes fastest.
Arguments:
- query_pool: bfloat16 [16384, 4096], P(('qr', 'pc')), may hold values from -14 to 14
- passage_pool: bfloat16 [16384, 4096], P(('pc', 'qr')), may hold values from -14 to 14
- proj: bfloat16 [4096, 1024], replicated, may hold values from -0.09375 to 0.09375
- positive: int32 [16384], P(('qr', 'pc')), may hold values from 0 to 16383, as said below
Outputs:
- loss: float32 [], replicated
- grad_query_pool: float32 [16384, 4096], P(('qr', 'pc'))
- grad_passage_pool: float32 [16384, 4096], P(('pc', 'qr'))
The draws below stay inside these ranges and needn't reach their ends.
Inputs may be any that keep to these rules, and one draw needn't show every extreme that they name: Every passage is the positive of exactly one query.
All inputs are finite; a program needn't handle non-finite values.
Results may differ from the reference program's by a relative error of at most 0.023.
Values may be sent and summed in bfloat16 or wider, within the bound.
No kernel may reach another device: no remote copies, remote signals or barrier semaphores. Data moves between devices by JAX's collectives and lax.ppermute only.
A program may use at most 64 MiB of HBM per device.

```python
import jax
import jax.numpy as jnp
from jax import lax

D = 4096
E = 1024
PAIRS_DEV = 64
PAIRS = 16384
N_QR = 16
N_PC = 16


topic_count = 16


def shared_topics(key):
    return jax.random.truncated_normal(key, -4.0, 4.0, (topic_count, D), jnp.float32)


def topic_rows(key, topics, amp_low, amp_high, noise_limit):
    keys = jax.random.split(key, 4)
    picks = jax.random.randint(keys[0], (PAIRS,), 0, topic_count)
    signs = (2 * jax.random.randint(keys[1], (PAIRS, 1), 0, 2) - 1).astype(jnp.float32)
    amplitude = jnp.exp(jax.random.uniform(keys[2], (PAIRS, 1), jnp.float32, jnp.log(amp_low), jnp.log(amp_high)))
    noise = jax.random.truncated_normal(keys[3], -noise_limit, noise_limit, (PAIRS, D), jnp.float32)
    return amplitude * signs * topics[picks] + noise


def pair_positive(key):
    key = jax.random.fold_in(key, 3)
    keys = jax.random.split(key, 2)
    order = jax.random.permutation(keys[0], PAIRS).astype(jnp.int32)
    half = PAIRS // 2
    first_half = order[:half]
    second_half = order[half:2 * half]
    swapped = jax.random.randint(keys[1], (half,), 0, 4) == 0
    result = jnp.arange(PAIRS, dtype=jnp.int32)
    result = result.at[first_half].set(jnp.where(swapped, second_half, first_half))
    result = result.at[second_half].set(jnp.where(swapped, first_half, second_half))
    return result


def mixed_passages(own_rows, query_rows, positive, weight):
    weight_at = jnp.zeros((PAIRS,), jnp.float32).at[positive].set(weight)
    query_at = jnp.zeros((PAIRS, D), jnp.float32).at[positive].set(query_rows)
    return (own_rows + weight_at[:, None] * query_at) / (1.0 + weight_at[:, None])


def draw_query_pool(key, part):
    topics = shared_topics(key)
    key = jax.random.fold_in(key, 1)
    return topic_rows(key, topics, 0.5, 2.5, 4.0).astype(jnp.bfloat16)


def draw_passage_pool(key, part):
    topics = shared_topics(key)
    positive = pair_positive(key)
    query_key = jax.random.fold_in(key, 1)
    key = jax.random.fold_in(key, 2)
    fraction = jnp.arange(PAIRS, dtype=jnp.float32) / PAIRS
    query_rows = topic_rows(query_key, topics, 0.5, 2.5, 4.0)
    own_rows = topic_rows(key, topics, 0.5, 2.5, 4.0)
    weight = 3.0 * fraction
    return mixed_passages(own_rows, query_rows, positive, weight).astype(jnp.bfloat16)


def draw_positive(key, part):
    return pair_positive(key)


def scatter_about(rng, dims, deviation, bound, kind=jnp.bfloat16):
    return jnp.clip(deviation * jax.random.normal(rng, dims, jnp.float32), -bound, bound).astype(kind)


def setup_inputs(seed: int = 0) -> dict:
    key_of = jax.random.split(jax.random.key(seed), 5)
    query_pool = draw_query_pool(jax.random.fold_in(key_of[4], 71), 0)
    passage_pool = draw_passage_pool(jax.random.fold_in(key_of[4], 71), 0)
    proj = scatter_about(key_of[2], (D, E), D ** -0.5, 0.09375)
    positive = draw_positive(jax.random.fold_in(key_of[4], 71), 0)
    return {"query_pool": query_pool, "passage_pool": passage_pool, "proj": proj, "positive": positive}


logit_scale = 20.0
grad_scale = 128.0
norm_eps = 1e-06

def embed_rows(pool, proj):
    raw_rows = jnp.dot(pool, proj, preferred_element_type=jnp.float32)
    inv_rows = lax.rsqrt(lax.optimization_barrier(jnp.sum(raw_rows * raw_rows, axis=-1, keepdims=True)) + norm_eps)
    return (raw_rows, inv_rows)

def normal_back(raw_rows, inv_rows, incoming):
    unit_rows = raw_rows * inv_rows
    return inv_rows * (incoming - unit_rows * lax.optimization_barrier(jnp.sum(unit_rows * incoming, axis=-1, keepdims=True)))

def reference(query_pool, passage_pool, proj, positive):
    raw_query, inv_query = embed_rows(query_pool, proj)
    raw_passage, inv_passage = embed_rows(passage_pool, proj)
    query_embed = (raw_query * inv_query).astype(jnp.bfloat16)
    passage_embed = (raw_passage * inv_passage).astype(jnp.bfloat16)
    block_rows = PAIRS_DEV * N_PC
    blocks = N_QR
    column_group = PAIRS_DEV * N_QR
    query_blocks = query_embed.reshape(blocks, block_rows, E)
    positive_blocks = positive.reshape(blocks, block_rows)
    passage_groups = passage_embed.astype(jnp.float32).reshape(N_PC, column_group, E)

    def block_logits(query_block):
        return logit_scale * lax.dot_general(query_block, passage_embed, (((1,), (1,)), ((), ())), preferred_element_type=jnp.float32)

    def first_pass(column_acc, element):
        query_block, index_block = element
        logits = block_logits(query_block)
        shifted = jnp.exp(logits - logit_scale)
        picked = jnp.take_along_axis(logits, index_block[:, None], axis=1)[:, 0]
        return (column_acc + lax.optimization_barrier(jnp.sum(shifted, axis=0)), (lax.optimization_barrier(jnp.sum(shifted, axis=1)), picked))
    column_sum, (row_sum, picked) = lax.scan(first_pass, jnp.zeros((PAIRS,), jnp.float32), (query_blocks, positive_blocks))
    row_lse = logit_scale + jnp.log(row_sum)
    column_lse = logit_scale + jnp.log(column_sum)
    loss = (jnp.sum(row_lse) + jnp.sum(column_lse) - 2.0 * jnp.sum(picked)) / (2.0 * PAIRS)

    def second_pass(passage_acc, element):
        query_block, index_block, lse_block = element
        logits = block_logits(query_block)
        onehot = (lax.broadcasted_iota(jnp.int32, logits.shape, 1) == index_block[:, None]).astype(jnp.float32)
        grad_tile = grad_scale * (0.5 * (jnp.exp(logits - lse_block[:, None]) + jnp.exp(logits - column_lse[None, :])) - onehot)
        grad_tile = grad_tile.astype(jnp.bfloat16)
        grad_groups = grad_tile.astype(jnp.float32).reshape(block_rows, N_PC, column_group)
        query_terms = logit_scale * jnp.einsum('rgc,gce->gre', grad_groups, passage_groups, precision=lax.Precision.HIGHEST)
        query_grad = lax.optimization_barrier(jnp.sum(query_terms.astype(jnp.bfloat16).astype(jnp.float32), axis=0))
        passage_term = logit_scale * lax.dot_general(grad_tile, query_block, (((0,), (0,)), ((), ())), preferred_element_type=jnp.float32)
        passage_term = passage_term.astype(jnp.bfloat16).astype(jnp.float32)
        return (passage_acc + passage_term, query_grad)
    passage_sum, query_grads = lax.scan(second_pass, jnp.zeros((PAIRS, E), jnp.float32), (query_blocks, positive_blocks, row_lse.reshape(blocks, block_rows)))
    grad_query_embed = query_grads.reshape(PAIRS, E)
    grad_passage_embed = passage_sum
    grad_raw_query = normal_back(raw_query, inv_query, grad_query_embed).astype(jnp.bfloat16)
    grad_raw_passage = normal_back(raw_passage, inv_passage, grad_passage_embed).astype(jnp.bfloat16)
    grad_query_pool = lax.dot_general(grad_raw_query, proj, (((1,), (1,)), ((), ())), preferred_element_type=jnp.float32)
    grad_passage_pool = lax.dot_general(grad_raw_passage, proj, (((1,), (1,)), ((), ())), preferred_element_type=jnp.float32)
    return (loss, grad_query_pool, grad_passage_pool)
```

```python
import jax
import jax.numpy as jnp
from jax import lax
from jax.sharding import Mesh, PartitionSpec as P

logit_scale = 20.0
grad_scale = 128.0
norm_eps = 1e-06

NY, NX, NZ, NC = 4, 4, 8, 2
QR = ("y", "x")
PC = ("z", "c")
f32 = jnp.float32
bf16 = jnp.bfloat16


def shift(value, axis, size, step):
    return lax.ppermute(value, axis, [(i, (i + step) % size) for i in range(size)])


def swap(value, axis, size, bit):
    return lax.ppermute(value, axis, [(i, i ^ bit) for i in range(size)])


pc_steps = (("c", NC, 1), ("z", NZ, 1), ("z", NZ, 2), ("z", NZ, 4))
qr_steps = (("x", NX, 1), ("x", NX, 2), ("y", NY, 1), ("y", NY, 2))


def embed_rows(pool, proj):
    raw_rows = jnp.dot(pool, proj, preferred_element_type=f32)
    inv_rows = lax.rsqrt(jnp.sum(raw_rows * raw_rows, axis=-1, keepdims=True) + norm_eps)
    return (raw_rows, inv_rows)


def normal_back(raw_rows, inv_rows, incoming):
    unit_rows = raw_rows * inv_rows
    return inv_rows * (incoming - unit_rows * jnp.sum(unit_rows * incoming, axis=-1, keepdims=True))


def scatter_z(blocks, z_index):
    def block(k):
        return lax.dynamic_index_in_dim(blocks, (z_index + k) % NZ, 0, keepdims=False)

    far = block(NZ // 2)
    half = far.shape[0] // 2
    down = shift(far[:half], "z", NZ, -1)
    up = shift(far[half:], "z", NZ, 1)
    down = jnp.concatenate([down.astype(f32), jnp.zeros(down.shape, f32)], axis=0)
    up = jnp.concatenate([jnp.zeros(up.shape, f32), up.astype(f32)], axis=0)
    for k in range(NZ // 2 - 1, 0, -1):
        down = shift((block(NZ - k).astype(f32) + down).astype(bf16), "z", NZ, -1).astype(f32)
        up = shift((block(k).astype(f32) + up).astype(bf16), "z", NZ, 1).astype(f32)
    return block(0).astype(f32) + down + up


def body(query_pool, passage_pool, proj, positive):
    z_index = lax.axis_index("z")
    c_index = lax.axis_index("c")
    pc_index = z_index * NC + c_index
    own_rows = query_pool.shape[0]
    raw_query, inv_query = embed_rows(query_pool, proj)
    query_embed = (raw_query * inv_query).astype(bf16)
    query_tile = lax.all_gather(query_embed, PC, axis=0, tiled=True)
    raw_passage, inv_passage = embed_rows(passage_pool, proj)
    passage_embed = (raw_passage * inv_passage).astype(bf16)
    passage_tile = lax.all_to_all(jnp.tile(passage_embed, (NY * NX, 1)), QR, 0, 0, tiled=True)
    positive_tile = lax.all_gather(positive, PC, axis=0, tiled=True)
    tile_rows = query_tile.shape[0]
    tile_cols = passage_tile.shape[0]
    width = query_tile.shape[1]
    logits = logit_scale * lax.dot_general(
        query_tile, passage_tile, (((1,), (1,)), ((), ())), preferred_element_type=f32
    )
    shifted = jnp.exp(logits - logit_scale)
    row_sum = jnp.sum(shifted, axis=1)
    column_sum = jnp.sum(shifted, axis=0)
    for pc_step, qr_step in zip(pc_steps, qr_steps):
        row_sum = row_sum + swap(row_sum, *pc_step)
        column_sum = column_sum + swap(column_sum, *qr_step)
    row_lse = logit_scale + jnp.log(row_sum)
    column_lse = logit_scale + jnp.log(column_sum)
    local_column = positive_tile - pc_index * tile_cols
    onehot = lax.broadcasted_iota(jnp.int32, logits.shape, 1) == local_column[:, None]
    positive_sum = jnp.sum(jnp.where(onehot, logits, 0.0))
    loss = (
        jnp.sum(row_lse) / (NZ * NC) + jnp.sum(column_lse) / (NY * NX) - 2.0 * positive_sum
    ).reshape(1)
    for step in pc_steps + qr_steps:
        loss = loss + swap(loss, *step)
    loss = loss[0] / (2.0 * tile_rows * NY * NX)
    grad_tile = grad_scale * (
        0.5 * (jnp.exp(logits - row_lse[:, None]) + jnp.exp(logits - column_lse[None, :]))
        - onehot.astype(f32)
    )
    grad_tile = grad_tile.astype(bf16)
    query_partial = (
        logit_scale * jnp.dot(grad_tile, passage_tile, preferred_element_type=f32)
    ).astype(bf16)
    passage_partial = (
        logit_scale
        * lax.dot_general(
            grad_tile, query_tile, (((0,), (0,)), ((), ())), preferred_element_type=f32
        )
    ).astype(bf16)
    passage_terms = lax.all_to_all(passage_partial, QR, 0, 0, tiled=True)
    grad_passage_embed = jnp.sum(
        passage_terms.reshape(NY * NX, own_rows, width).astype(f32), axis=0
    )
    query_parts = query_partial.reshape(NZ, NC, own_rows, width)
    other = swap(lax.dynamic_index_in_dim(query_parts, 1 - c_index, 1, keepdims=False), "c", NC, 1)
    own = lax.dynamic_index_in_dim(query_parts, c_index, 1, keepdims=False)
    blocks = (own.astype(f32) + other.astype(f32)).astype(bf16)
    grad_query_embed = scatter_z(blocks, z_index)
    grad_raw_query = normal_back(raw_query, inv_query, grad_query_embed).astype(bf16)
    grad_raw_passage = normal_back(raw_passage, inv_passage, grad_passage_embed).astype(bf16)
    grad_query_pool = lax.dot_general(
        grad_raw_query, proj, (((1,), (1,)), ((), ())), preferred_element_type=f32
    )
    grad_passage_pool = lax.dot_general(
        grad_raw_passage, proj, (((1,), (1,)), ((), ())), preferred_element_type=f32
    )
    return (loss, grad_query_pool, grad_passage_pool)


def solution(mesh):
    fine = Mesh(mesh.devices.reshape(NY, NX, NZ, NC), ("y", "x", "z", "c"))
    in_specs = (
        P(("y", "x", "z", "c"), None),
        P(("z", "c", "y", "x"), None),
        P(),
        P(("y", "x", "z", "c")),
    )
    out_specs = (P(), P(("y", "x", "z", "c"), None), P(("z", "c", "y", "x"), None))
    return jax.shard_map(
        body, mesh=fine, in_specs=in_specs, out_specs=out_specs, check_vma=False
    )
```

```python
import functools

import jax
import jax.numpy as jnp
from jax import lax
from jax.experimental import pallas as pl
from jax.experimental.pallas import tpu as pltpu
from jax.sharding import Mesh, PartitionSpec as P

logit_scale = 20.0
grad_scale = 128.0
norm_eps = 1e-06
log2_e = 1.4426950408889634

NY, NX, NZ, NC = 4, 4, 8, 2
QR = ("y", "x")
PC = ("z", "c")
f32 = jnp.float32
bf16 = jnp.bfloat16
LANES = 128
HBM = pl.BlockSpec(memory_space=pltpu.HBM)
VMEM = pl.BlockSpec(memory_space=pltpu.VMEM)
SMEM = pl.BlockSpec(memory_space=pltpu.SMEM)
params = pltpu.CompilerParams(vmem_limit_bytes=32 * 1024 * 1024)
NT = (((1,), (1,)), ((), ()))
TN = (((0,), (0,)), ((), ()))


def shift(value, axis, size, step):
    return lax.ppermute(value, axis, [(i, (i + step) % size) for i in range(size)])


def swap(value, axis, size, bit):
    return lax.ppermute(value, axis, [(i, i ^ bit) for i in range(size)])


pc_steps = (("c", NC, 1), ("z", NZ, 1), ("z", NZ, 2), ("z", NZ, 4))
qr_steps = (("x", NX, 1), ("x", NX, 2), ("y", NY, 1), ("y", NY, 2))


def sds(shape, dtype):
    return jax.ShapeDtypeStruct(shape, dtype)


def fixed(shape):
    return pl.BlockSpec(shape, lambda *i: (0,) * len(shape))


def embed_kernel(
    query_ref,
    passage_ref,
    proj_ref,
    positive_ref,
    message_ref,
    copies_ref,
    unit_ref,
    inv_ref,
    pools,
    weights,
    spread,
    in_sems,
    out_sems,
):
    rows, depth = query_ref.shape
    width = proj_ref.shape[1]
    steps = in_sems.shape[0] - 2
    chunk = depth // steps
    loads = [
        pltpu.make_async_copy(query_ref, pools.at[:rows], in_sems.at[0]),
        pltpu.make_async_copy(passage_ref, pools.at[rows:], in_sems.at[1]),
    ]
    for k in range(steps):
        part = pl.ds(k * chunk, chunk)
        loads.append(pltpu.make_async_copy(proj_ref.at[part], weights.at[part], in_sems.at[k + 2]))
    for load in loads:
        load.start()
    loads[0].wait()
    loads[1].wait()
    raw = jnp.zeros((2 * rows, width), f32)
    for k in range(steps):
        loads[k + 2].wait()
        part = pl.ds(k * chunk, chunk)
        raw = raw + jnp.dot(pools[:, part], weights[part, :], preferred_element_type=f32)
    inv = lax.rsqrt(jnp.sum(raw * raw, axis=-1, keepdims=True) + norm_eps)
    unit = raw * inv
    embed = unit.astype(bf16)
    spread[...] = embed[rows:]
    stores = []
    for k in range(copies_ref.shape[0] // rows):
        part = pl.ds(k * rows, rows)
        stores.append(pltpu.make_async_copy(spread, copies_ref.at[part], out_sems.at[k]))
    for store in stores:
        store.start()
    unit_ref[...] = unit
    inv_ref[...] = jnp.broadcast_to(inv, inv_ref.shape)
    message_ref[:, :width] = embed[:rows]
    square = (rows, rows)
    line = jnp.broadcast_to(positive_ref[...].astype(f32), square)
    on = lax.broadcasted_iota(jnp.int32, square, 0) == lax.broadcasted_iota(jnp.int32, square, 1)
    index = jnp.sum(jnp.where(on, line, 0.0), axis=1, keepdims=True)
    high = jnp.floor(index * (1.0 / LANES))
    low = index - high * LANES
    lane = lax.broadcasted_iota(jnp.int32, (rows, LANES), 1)
    message_ref[:, width:] = jnp.where(lane == 0, high, jnp.where(lane == 1, low, 0.0)).astype(bf16)
    for store in stores:
        store.wait()


def embed(query_pool, passage_pool, proj, positive):
    rows, depth = query_pool.shape
    width = proj.shape[1]
    copies = NY * NX
    steps = 8
    return pl.pallas_call(
        embed_kernel,
        in_specs=[HBM, HBM, HBM, VMEM],
        out_specs=[VMEM, HBM, VMEM, VMEM],
        out_shape=[
            sds((rows, width + LANES), bf16),
            sds((copies * rows, width), bf16),
            sds((2 * rows, width), f32),
            sds((2 * rows, LANES), f32),
        ],
        scratch_shapes=[
            pltpu.VMEM((2 * rows, depth), bf16),
            pltpu.VMEM((depth, width), bf16),
            pltpu.VMEM((rows, width), bf16),
            pltpu.SemaphoreType.DMA((steps + 2,)),
            pltpu.SemaphoreType.DMA((copies,)),
        ],
        compiler_params=params,
        name="embed",
    )(query_pool, passage_pool, proj, positive)


def positive_column(query_ref, width, place_ref, columns):
    parts = query_ref[:, width:].astype(f32)
    index = parts[:, 0:1] * LANES + parts[:, 1:2]
    first = (place_ref[0] * NC + place_ref[1]) * columns
    return index.astype(jnp.int32) - first


def line_of(place_ref, k):
    z = lax.rem(place_ref[0] + k % NZ, NZ)
    c = place_ref[1] if k < NZ else 1 - place_ref[1]
    return pl.ds(c * NZ + z, 1)


def logits_kernel(place_ref, *refs):
    pieces = refs[: NZ * NC]
    passage_ref, exp_ref, query_ref, kept_ref, row_ref, col_ref, row_acc, in_sems = refs[NZ * NC :]
    own = pieces[0].shape[0]
    columns, width = passage_ref.shape
    rows = query_ref.shape[0]
    steps = in_sems.shape[0] - NZ * NC
    chunk = columns // steps
    loads = []
    for k, piece in enumerate(pieces):
        loads.append(pltpu.make_async_copy(piece, query_ref.at[pl.ds(k * own, own)], in_sems.at[k]))
    for k in range(steps):
        part = pl.ds(k * chunk, chunk)
        sem = in_sems.at[NZ * NC + k]
        loads.append(pltpu.make_async_copy(passage_ref.at[part], kept_ref.at[part], sem))
    for load in loads:
        load.start()
    for load in loads[: NZ * NC]:
        load.wait()
    positive = positive_column(query_ref, width, place_ref, columns)
    row_part = jnp.zeros((rows, LANES), f32)
    picked = jnp.zeros((1, chunk), f32)
    for k in range(steps):
        loads[NZ * NC + k].wait()
        part = pl.ds(k * chunk, chunk)
        dots = lax.dot_general(
            query_ref[:, :width], kept_ref[part, :], NT, preferred_element_type=f32
        )
        shifted = jnp.exp2(dots * (logit_scale * log2_e) - logit_scale * log2_e)
        exp_ref[:, part] = shifted
        col_ref[:, part] = jnp.sum(shifted, axis=0, keepdims=True)
        for n in range(chunk // LANES):
            row_part = row_part + shifted[:, n * LANES : (n + 1) * LANES]
        column = lax.broadcasted_iota(jnp.int32, (rows, chunk), 1) + k * chunk
        found = jnp.where(column == positive, dots, 0.0)
        picked = picked + jnp.sum(found, axis=0, keepdims=True)
    total = logit_scale * jnp.sum(picked, axis=1, keepdims=True)
    row_acc[...] = row_part
    lane = lax.broadcasted_iota(jnp.int32, (1, LANES), 1)
    for k in range(0, NZ * NC, 2):
        turned = row_acc[k * own : (k + 2) * own, :].T
        line = jnp.sum(turned, axis=0, keepdims=True)
        row_ref[line_of(place_ref, k), :] = jnp.where(lane < own, line, total)
        line = pltpu.roll(line, own, 1)
        row_ref[line_of(place_ref, k + 1), :] = jnp.where(lane < own, line, total)


def tile_logits(place, pieces, passage_tile):
    own, wide = pieces[0].shape
    columns, width = passage_tile.shape
    rows = own * len(pieces)
    steps = 4
    return pl.pallas_call(
        logits_kernel,
        in_specs=[SMEM] + [HBM] * (len(pieces) + 1),
        out_specs=[VMEM] * 5,
        out_shape=[
            sds((rows, columns), f32),
            sds((rows, wide), bf16),
            sds((columns, width), bf16),
            sds((len(pieces), LANES), f32),
            sds((1, columns), f32),
        ],
        scratch_shapes=[
            pltpu.VMEM((rows, LANES), f32),
            pltpu.SemaphoreType.DMA((len(pieces) + steps,)),
        ],
        compiler_params=params,
        name="logits",
    )(place, *pieces, passage_tile)


def grads_kernel(
    place_ref,
    exp_ref,
    row_ref,
    col_ref,
    query_ref,
    passage_ref,
    part_ref,
    own_ref,
    other_ref,
    col_loss_ref,
    grad,
    row_scale,
    parts,
    sems,
):
    columns, width = passage_ref.shape
    rows = query_ref.shape[0]
    own = rows // (NZ * NC)
    steps = sems.shape[0]
    chunk = columns // steps
    half = 0.5 * grad_scale
    lane = lax.broadcasted_iota(jnp.int32, (1, LANES), 1)
    row_total = logit_scale * rows - 2.0 * row_ref[0:1, own : own + 1]
    for k in range(0, NZ * NC, 2):
        first, second = row_ref[line_of(place_ref, k), :], row_ref[line_of(place_ref, k + 1), :]
        line = jnp.where(lane < own, first, pltpu.roll(second, own, 1))
        row_total = row_total + jnp.sum(jnp.log(line), axis=1, keepdims=True)
        turned = jnp.broadcast_to(half / line, (LANES, LANES)).T
        row_scale[k * own : (k + 2) * own, :] = turned
    col_total = jnp.sum(jnp.log(col_ref[...]), axis=1, keepdims=True) + logit_scale * columns
    col_loss_ref[...] = jnp.broadcast_to(col_total, (1, LANES))
    high = row_total.astype(bf16).astype(f32)
    middle = (row_total - high).astype(bf16).astype(f32)
    low = row_total - high - middle
    extra = jnp.where(lane == 0, high, jnp.where(lane == 1, middle, jnp.where(lane == 2, low, 0.0)))
    extra = jnp.broadcast_to(extra, (chunk, LANES)).astype(bf16)
    positive = positive_column(query_ref, width, place_ref, columns)
    stores = []
    for k in range(steps):
        part = pl.ds(k * chunk, chunk)
        scale = jnp.concatenate([row_scale[...]] * (chunk // LANES), axis=1)
        scale = scale + half / col_ref[:, part]
        column = lax.broadcasted_iota(jnp.int32, (rows, chunk), 1) + k * chunk
        hit = jnp.where(column == positive, grad_scale, 0.0)
        tile = (exp_ref[:, part] * scale - hit).astype(bf16)
        grad[:, part] = tile
        term = lax.dot_general(tile, query_ref[:, :width], TN, preferred_element_type=f32)
        parts[part, :width] = (logit_scale * term).astype(bf16)
        parts[part, width:] = extra
        stores.append(pltpu.make_async_copy(parts.at[part], part_ref.at[part], sems.at[k]))
        stores[-1].start()
    for k, out_ref in enumerate((own_ref, other_ref)):
        part = pl.ds(k * NZ * own, NZ * own)
        term = jnp.dot(grad[part, :], passage_ref[...], preferred_element_type=f32)
        out_ref[...] = (logit_scale * term).astype(bf16).reshape(out_ref.shape)
    for store in stores:
        store.wait()


def tile_grads(place, shifted, row_sum, column_sum, query_tile, passage_tile):
    rows, wide = query_tile.shape
    columns, width = passage_tile.shape
    own = rows // (NZ * NC)
    steps = 4
    return pl.pallas_call(
        grads_kernel,
        in_specs=[SMEM] + [VMEM] * 5,
        out_specs=[HBM, VMEM, VMEM, VMEM],
        out_shape=[
            sds((columns, wide), bf16),
            sds((NZ, own, width), bf16),
            sds((NZ, own, width), bf16),
            sds((1, LANES), f32),
        ],
        scratch_shapes=[
            pltpu.VMEM((rows, columns), bf16),
            pltpu.VMEM((rows, LANES), f32),
            pltpu.VMEM((columns, wide), bf16),
            pltpu.SemaphoreType.DMA((steps,)),
        ],
        compiler_params=params,
        name="grads",
    )(place, shifted, row_sum, column_sum, query_tile, passage_tile)


def ring_step(own, other, turns, loss, came_loss):
    _, height, width = own.shape
    operands, in_specs, kept = [], [], []
    for block, came in turns:
        spec = pl.BlockSpec((1, height, width), lambda i, block=block: (block, 0, 0))
        operands += [own, other]
        in_specs += [spec, spec]
        kept.append(came is not None)
        if came is not None:
            operands.append(came)
            in_specs.append(fixed((height, width)))
    operands += [loss, came_loss]
    in_specs += [fixed((1, LANES))] * 2

    def kernel(*refs):
        refs = list(refs)
        outs = refs[len(operands) :]
        for out, there in zip(outs, kept):
            total = refs.pop(0)[0].astype(f32) + refs.pop(0)[0].astype(f32)
            if there:
                total = total + refs.pop(0)[...].astype(f32)
            out[...] = total.astype(out.dtype)
        outs[-1][...] = refs[0][...] + refs[1][...]

    count = len(turns)
    return pl.pallas_call(
        kernel,
        grid=(1,),
        in_specs=in_specs,
        out_specs=[fixed((height, width))] * count + [fixed((1, LANES))],
        out_shape=[sds((height, width), bf16)] * count + [sds((1, LANES), f32)],
        compiler_params=params,
        name="ring",
    )(*operands)


def final_kernel(
    count,
    base_ref,
    down_ref,
    up_ref,
    loss_ref,
    unit_ref,
    inv_ref,
    proj_ref,
    terms_ref,
    total_ref,
    query_ref,
    passage_ref,
    terms,
    raw,
    outs,
    in_sems,
    out_sems,
):
    rows, width = down_ref.shape
    steps = out_sems.shape[0] // 2
    chunk = proj_ref.shape[0] // steps
    loads = []
    blocks = in_sems.shape[0]
    height = terms_ref.shape[0] // blocks
    for k in range(blocks):
        part = pl.ds(k * height, height)
        loads.append(pltpu.make_async_copy(terms_ref.at[part], terms.at[part], in_sems.at[k]))
        loads[-1].start()

    def back(k, incoming):
        unit = unit_ref[k * rows : (k + 1) * rows, :]
        inv = inv_ref[k * rows : (k + 1) * rows, :1]
        along = jnp.sum(unit * incoming, axis=-1, keepdims=True)
        raw[k * rows : (k + 1) * rows, :] = (inv * (incoming - unit * along)).astype(bf16)

    back(0, base_ref[...].astype(f32) + down_ref[...].astype(f32) + up_ref[...].astype(f32))
    passage = jnp.zeros((rows, width), f32)
    total = loss_ref[:, :1]
    for k in range(blocks):
        loads[k].wait()
        for n in range(k * height, (k + 1) * height, rows):
            passage = passage + terms[n : n + rows, :width].astype(f32)
            extra = terms[n : n + 16, width:].astype(f32)[:1]
            total = total + jnp.sum(extra, axis=1, keepdims=True)
    total_ref[...] = total * (1.0 / count)
    back(1, passage)
    stores = []
    for k in range(steps):
        part = pl.ds(k * chunk, chunk)
        outs[:, part] = lax.dot_general(raw[...], proj_ref[part, :], NT, preferred_element_type=f32)
        for n, out_ref in enumerate((query_ref, passage_ref)):
            source = outs.at[pl.ds(n * rows, rows), part]
            store = pltpu.make_async_copy(source, out_ref.at[:, part], out_sems.at[2 * k + n])
            store.start()
            stores.append(store)
    for store in stores:
        store.wait()


def final(count, base, down, up, loss, unit, inv, proj, terms):
    rows, width = down.shape
    depth = proj.shape[0]
    steps = 4
    return pl.pallas_call(
        functools.partial(final_kernel, count),
        in_specs=[VMEM] * 7 + [HBM],
        out_specs=[VMEM, HBM, HBM],
        out_shape=[sds((1, 1), f32)] + [sds((rows, depth), f32)] * 2,
        scratch_shapes=[
            pltpu.VMEM(terms.shape, bf16),
            pltpu.VMEM((2 * rows, width), bf16),
            pltpu.VMEM((2 * rows, depth), f32),
            pltpu.SemaphoreType.DMA((4,)),
            pltpu.SemaphoreType.DMA((2 * steps,)),
        ],
        compiler_params=params,
        name="final",
    )(base, down, up, loss, unit, inv, proj, terms)


def gather_queries(message):
    pieces = {0: message}
    down = up = message
    for k in range(1, NZ // 2 + 1):
        down = shift(down, "z", NZ, -1)
        pieces[k] = down
        if k < NZ // 2:
            up = shift(up, "z", NZ, 1)
            pieces[NZ - k] = up
    own = [pieces[k] for k in range(NZ)]
    return own + [swap(piece, "c", NC, 1) for piece in own]


def body(query_pool, passage_pool, proj, positive):
    place = jnp.stack([lax.axis_index("z"), lax.axis_index("c")]).astype(jnp.int32)
    message, copies, unit, inv = embed(query_pool, passage_pool, proj, positive[None])
    passage_tile = lax.all_to_all(copies, QR, 0, 0, tiled=True)
    pieces = gather_queries(message)
    shifted, query_tile, passage_tile, row_sum, column_sum = tile_logits(
        place, pieces, passage_tile
    )
    for pc_step, qr_step in zip(pc_steps, qr_steps):
        row_sum = row_sum + swap(row_sum, *pc_step)
        column_sum = column_sum + swap(column_sum, *qr_step)
    partial, own, other, loss = tile_grads(
        place, shifted, row_sum, column_sum, query_tile, passage_tile
    )
    terms = lax.all_to_all(partial, QR, 0, 0, tiled=True)
    other = swap(other, "c", NC, 1)
    down, loss = ring_step(own, other, [(4, None)], loss, swap(loss, *pc_steps[0]))
    came = shift(down, "z", NZ, -1)
    turns = [(5, came), (3, None)]
    down, up, loss = ring_step(own, other, turns, loss, swap(loss, *pc_steps[1]))
    came = shift(down, "z", NZ, -1), shift(up, "z", NZ, 1)
    turns = [(6, came[0]), (2, came[1])]
    down, up, loss = ring_step(own, other, turns, loss, swap(loss, *pc_steps[2]))
    came = shift(down, "z", NZ, -1), shift(up, "z", NZ, 1)
    turns = [(7, came[0]), (1, came[1]), (0, None)]
    down, up, base, loss = ring_step(own, other, turns, loss, swap(loss, *pc_steps[3]))
    down, up = shift(down, "z", NZ, -1), shift(up, "z", NZ, 1)
    count = 2.0 * column_sum.shape[1] * NZ * NC
    total, grad_query_pool, grad_passage_pool = final(
        count, base, down, up, loss, unit, inv, proj, terms
    )
    return (total.reshape(()), grad_query_pool, grad_passage_pool)


def solution(mesh):
    fine = Mesh(mesh.devices.reshape(NY, NX, NZ, NC), ("y", "x", "z", "c"))
    in_specs = (
        P(("y", "x", "z", "c"), None),
        P(("z", "c", "y", "x"), None),
        P(),
        P(("y", "x", "z", "c")),
    )
    out_specs = (P(), P(("y", "x", "z", "c"), None), P(("z", "c", "y", "x"), None))
    return jax.shard_map(
        body, mesh=fine, in_specs=in_specs, out_specs=out_specs, check_vma=False
    )
```

```python
import functools

import jax
import jax.numpy as jnp
from jax import lax
from jax.experimental import pallas as pl
from jax.experimental.pallas import tpu as pltpu
from jax.sharding import Mesh, PartitionSpec as P

logit_scale = 20.0
grad_scale = 128.0
norm_eps = 1e-06
log2_e = 1.4426950408889634

NY, NX, NZ, NC = 4, 4, 8, 2
QR = ("y", "x")
PC = ("z", "c")
f32 = jnp.float32
bf16 = jnp.bfloat16
LANES = 128
EXTRA = 16
HBM = pl.BlockSpec(memory_space=pltpu.HBM)
VMEM = pl.BlockSpec(memory_space=pltpu.VMEM)
params = pltpu.CompilerParams(vmem_limit_bytes=24 * 1024 * 1024)
NT = (((1,), (1,)), ((), ()))
TN = (((0,), (0,)), ((), ()))


def shift(value, axis, size, step):
    return lax.ppermute(value, axis, [(i, (i + step) % size) for i in range(size)])


def swap(value, axis, size, bit):
    return lax.ppermute(value, axis, [(i, i ^ bit) for i in range(size)])


pc_steps = (("c", NC, 1), ("z", NZ, 1), ("z", NZ, 2), ("z", NZ, 4))
qr_steps = (("x", NX, 1), ("x", NX, 2), ("y", NY, 1), ("y", NY, 2))


def sds(shape, dtype):
    return jax.ShapeDtypeStruct(shape, dtype)


def in_hbm(value):
    return pltpu.with_memory_space_constraint(value, pltpu.HBM)


def in_vmem(value):
    return pltpu.with_memory_space_constraint(value, pltpu.VMEM)


def fixed(shape):
    return pl.BlockSpec(shape, lambda *i: (0,) * len(shape))


def embed_kernel(
    query_ref,
    passage_ref,
    proj_ref,
    positive_ref,
    message_ref,
    copies_ref,
    state_ref,
    weights,
    pools,
    indices,
    spread,
    state,
    in_sems,
    out_sems,
):
    rows, depth = query_ref.shape
    width = proj_ref.shape[1]
    steps = in_sems.shape[0] - 3
    chunk = depth // steps
    loads = [
        pltpu.make_async_copy(query_ref, pools.at[:rows], in_sems.at[0]),
        pltpu.make_async_copy(passage_ref, pools.at[rows:], in_sems.at[1]),
    ]
    for k in range(steps):
        part = pl.ds(k * chunk, chunk)
        loads.append(pltpu.make_async_copy(proj_ref.at[part], weights.at[part], in_sems.at[k + 2]))
    loads.append(pltpu.make_async_copy(positive_ref, indices, in_sems.at[steps + 2]))
    for load in loads:
        load.start()
    loads[0].wait()
    loads[1].wait()
    raw = jnp.zeros((2 * rows, width), f32)
    for k in range(steps):
        loads[k + 2].wait()
        part = pl.ds(k * chunk, chunk)
        raw = raw + jnp.dot(pools[:, part], weights[part, :], preferred_element_type=f32)
    inv = lax.rsqrt(jnp.sum(raw * raw, axis=-1, keepdims=True) + norm_eps)
    unit = raw * inv
    embed = unit.astype(bf16)
    spread[...] = embed[rows:]
    stores = []
    for k in range(copies_ref.shape[0] // rows):
        part = pl.ds(k * rows, rows)
        stores.append(pltpu.make_async_copy(spread, copies_ref.at[part], out_sems.at[k]))
    for store in stores:
        store.start()
    state[:, :width] = unit
    state[:, width:] = jnp.broadcast_to(inv, (2 * rows, LANES))
    stores.append(pltpu.make_async_copy(state, state_ref, out_sems.at[len(stores)]))
    stores[-1].start()
    message_ref[:, :width] = embed[:rows]
    loads[-1].wait()
    square = (rows, rows)
    line = jnp.broadcast_to(indices[...].astype(f32), square)
    on = lax.broadcasted_iota(jnp.int32, square, 0) == lax.broadcasted_iota(jnp.int32, square, 1)
    index = jnp.sum(jnp.where(on, line, 0.0), axis=1, keepdims=True)
    high = jnp.floor(index * (1.0 / LANES))
    low = index - high * LANES
    lane = lax.broadcasted_iota(jnp.int32, (rows, LANES), 1)
    message_ref[:, width:] = jnp.where(lane == 0, high, jnp.where(lane == 1, low, 0.0)).astype(bf16)
    for store in stores:
        store.wait()


def embed(query_pool, passage_pool, proj, positive):
    rows, depth = query_pool.shape
    width = proj.shape[1]
    copies = NY * NX
    steps = 8
    return pl.pallas_call(
        embed_kernel,
        in_specs=[HBM] * 4,
        out_specs=[VMEM, HBM, HBM],
        out_shape=[
            sds((rows, width + LANES), bf16),
            pltpu.HBM((copies * rows, width), bf16),
            pltpu.HBM((2 * rows, width + LANES), f32),
        ],
        scratch_shapes=[
            pltpu.VMEM((depth, width), bf16),
            pltpu.VMEM((2 * rows, depth), bf16),
            pltpu.VMEM((1, rows), jnp.int32),
            pltpu.VMEM((rows, width), bf16),
            pltpu.VMEM((2 * rows, width + LANES), f32),
            pltpu.SemaphoreType.DMA((steps + 3,)),
            pltpu.SemaphoreType.DMA((copies + 1,)),
        ],
        compiler_params=params,
        name="embed",
    )(*map(in_hbm, (query_pool, passage_pool, proj, positive)))


def positive_column(query_ref, part, width, columns):
    words = query_ref[part, width:].astype(f32)
    index = words[:, 0:1] * LANES + words[:, 1:2]
    first = (lax.axis_index("z") * NC + lax.axis_index("c")) * columns
    return index.astype(jnp.int32) - first


def line_of(k):
    z = lax.rem(lax.axis_index("z") + k % NZ, NZ)
    c = lax.axis_index("c")
    return pl.ds((c if k < NZ else 1 - c) * NZ + z, 1)


def logits_kernel(*refs):
    pieces = refs[: NZ * NC]
    passage_ref, exp_ref, query_ref, row_ref, col_ref, row_acc, in_sems = refs[NZ * NC :]
    own = pieces[0].shape[0]
    columns, width = passage_ref.shape
    rows = query_ref.shape[0]
    loads = []
    for k, piece in enumerate(pieces):
        loads.append(pltpu.make_async_copy(piece, query_ref.at[pl.ds(k * own, own)], in_sems.at[k]))
        loads[-1].start()
    steps = 2
    each = rows // steps
    picked = jnp.zeros((1, columns), f32)
    col_sum = jnp.zeros((1, columns), f32)
    for k in range(steps):
        for load in loads[k * each // own : (k + 1) * each // own]:
            load.wait()
        part = pl.ds(k * each, each)
        positive = positive_column(query_ref, part, width, columns)
        dots = lax.dot_general(
            query_ref[part, :width], passage_ref[...], NT, preferred_element_type=f32
        )
        shifted = jnp.exp2(dots * (logit_scale * log2_e) - logit_scale * log2_e)
        exp_ref[part, :] = shifted
        col_sum = col_sum + jnp.sum(shifted, axis=0, keepdims=True)
        row_part = shifted[:, :LANES]
        for n in range(1, columns // LANES):
            row_part = row_part + shifted[:, n * LANES : (n + 1) * LANES]
        row_acc[part, :] = row_part
        column = lax.broadcasted_iota(jnp.int32, (each, columns), 1)
        found = jnp.where(column == positive, dots, 0.0)
        picked = picked + jnp.sum(found, axis=0, keepdims=True)
    col_ref[...] = col_sum
    total = logit_scale * jnp.sum(picked, axis=1, keepdims=True)
    lane = lax.broadcasted_iota(jnp.int32, (1, LANES), 1)
    for k in range(0, NZ * NC, 2):
        turned = row_acc[k * own : (k + 2) * own, :].T
        line = jnp.sum(turned, axis=0, keepdims=True)
        row_ref[line_of(k), :] = jnp.where(lane < own, line, total)
        line = pltpu.roll(line, own, 1)
        row_ref[line_of(k + 1), :] = jnp.where(lane < own, line, total)


def tile_logits(pieces, passage_tile):
    own, wide = pieces[0].shape
    columns, width = passage_tile.shape
    rows = own * len(pieces)
    return pl.pallas_call(
        logits_kernel,
        in_specs=[HBM] * len(pieces) + [VMEM],
        out_specs=[VMEM] * 4,
        out_shape=[
            pltpu.VMEM((rows, columns), f32),
            pltpu.VMEM((rows, wide), bf16),
            sds((len(pieces), LANES), f32),
            sds((1, columns), f32),
        ],
        scratch_shapes=[
            pltpu.VMEM((rows, LANES), f32),
            pltpu.SemaphoreType.DMA((len(pieces),)),
        ],
        compiler_params=params,
        name="logits",
    )(*map(in_hbm, pieces), in_vmem(passage_tile))


def in_thirds(value, shape):
    high = value.astype(bf16).astype(f32)
    middle = (value - high).astype(bf16).astype(f32)
    low = value - high - middle
    lane = lax.broadcasted_iota(jnp.int32, shape, 1)
    parts = jnp.where(lane == 1, middle, jnp.where(lane == 2, low, 0.0))
    return jnp.where(lane == 0, high, parts).astype(bf16)


def as_tiles(out_ref, block, extra):
    rows, width = block.shape
    for m in range(width // LANES):
        out_ref[m * rows : (m + 1) * rows, :] = block[:, m * LANES : (m + 1) * LANES]
    out_ref[width // LANES * rows :, :] = extra


def grads_kernel(
    exp_ref,
    row_ref,
    col_ref,
    query_ref,
    passage_ref,
    part_ref,
    own_ref,
    other_ref,
    grad,
    row_scale,
    parts,
    sems,
):
    columns, width = passage_ref.shape
    rows = query_ref.shape[0]
    own = rows // (NZ * NC)
    steps = sems.shape[0]
    chunk = columns // steps
    half = 0.5 * grad_scale
    lane = lax.broadcasted_iota(jnp.int32, (1, LANES), 1)
    row_total = logit_scale * rows - 2.0 * row_ref[0:1, own : own + 1]
    for k in range(0, NZ * NC, 2):
        first, second = row_ref[line_of(k), :], row_ref[line_of(k + 1), :]
        line = jnp.where(lane < own, first, pltpu.roll(second, own, 1))
        row_total = row_total + jnp.sum(jnp.log(line), axis=1, keepdims=True)
        turned = jnp.broadcast_to(half / line, (LANES, LANES)).T
        row_scale[k * own : (k + 2) * own, :] = turned
    col_total = jnp.sum(jnp.log(col_ref[...]), axis=1, keepdims=True) + logit_scale * columns
    row_extra = in_thirds(jnp.broadcast_to(row_total, (EXTRA, 1)), (EXTRA, LANES))
    col_extra = in_thirds(jnp.broadcast_to(col_total, (EXTRA, 1)), (EXTRA, LANES))
    positive = positive_column(query_ref, pl.ds(0, rows), width, columns)
    stores = []
    for k in range(steps):
        part = pl.ds(k * chunk, chunk)
        scale = jnp.concatenate([row_scale[...]] * (chunk // LANES), axis=1)
        scale = scale + half / col_ref[:, part]
        column = lax.broadcasted_iota(jnp.int32, (rows, chunk), 1) + k * chunk
        hit = jnp.where(column == positive, grad_scale, 0.0)
        tile = (exp_ref[:, part] * scale - hit).astype(bf16)
        grad[:, part] = tile
        term = lax.dot_general(tile, query_ref[:, :width], TN, preferred_element_type=f32)
        term = (logit_scale * term).astype(bf16)
        blocks = pl.ds(k * chunk // own, chunk // own)
        for n in range(chunk // own):
            as_tiles(parts.at[k * chunk // own + n], term[n * own : (n + 1) * own, :], row_extra)
        stores.append(pltpu.make_async_copy(parts.at[blocks], part_ref.at[blocks], sems.at[k]))
        stores[-1].start()
    for k, out_ref in enumerate((own_ref, other_ref)):
        part = pl.ds(k * NZ * own, NZ * own)
        term = jnp.dot(grad[part, :], passage_ref[...], preferred_element_type=f32)
        term = (logit_scale * term).astype(bf16)
        for n in range(NZ):
            as_tiles(out_ref.at[n], term[n * own : (n + 1) * own, :], col_extra)
    for store in stores:
        store.wait()


def tile_grads(shifted, row_sum, column_sum, query_tile, passage_tile):
    rows, wide = query_tile.shape
    columns, width = passage_tile.shape
    own = rows // (NZ * NC)
    block = (own * width // LANES + EXTRA, LANES)
    steps = 4
    return pl.pallas_call(
        grads_kernel,
        in_specs=[VMEM] * 5,
        out_specs=[HBM, VMEM, VMEM],
        out_shape=[
            pltpu.HBM((columns // own, *block), bf16),
            sds((NZ, *block), bf16),
            sds((NZ, *block), bf16),
        ],
        scratch_shapes=[
            pltpu.VMEM((rows, columns), bf16),
            pltpu.VMEM((rows, LANES), f32),
            pltpu.VMEM((columns // own, *block), bf16),
            pltpu.SemaphoreType.DMA((steps,)),
        ],
        compiler_params=params,
        name="grads",
    )(in_vmem(shifted), row_sum, column_sum, in_vmem(query_tile), in_vmem(passage_tile))


def ring_step(own, other, turns):
    _, height, width = own.shape
    operands, in_specs, kept = [], [], []
    for block, came in turns:
        spec = pl.BlockSpec((1, height, width), lambda i, block=block: (block, 0, 0))
        operands += [own, other]
        in_specs += [spec, spec]
        kept.append(came is not None)
        if came is not None:
            operands.append(came)
            in_specs.append(fixed((height, width)))

    def kernel(*refs):
        refs = list(refs)
        outs = refs[len(operands) :]
        for out, there in zip(outs, kept):
            total = refs.pop(0)[0].astype(f32) + refs.pop(0)[0].astype(f32)
            if there:
                total = total + refs.pop(0)[...].astype(f32)
            out[: height - EXTRA, :] = total[: height - EXTRA].astype(bf16)
            extra = jnp.sum(total[height - EXTRA :], axis=1, keepdims=True)
            out[height - EXTRA :, :] = in_thirds(extra, (EXTRA, LANES))

    count = len(turns)
    return pl.pallas_call(
        kernel,
        grid=(1,),
        in_specs=in_specs,
        out_specs=[fixed((height, width))] * count,
        out_shape=[sds((height, width), bf16)] * count,
        compiler_params=params,
        cost_estimate=pl.CostEstimate(flops=1, bytes_accessed=1, transcendentals=0),
        name="ring",
    )(*operands)


def final_kernel(
    count,
    own_ref,
    other_ref,
    down_ref,
    up_ref,
    proj_ref,
    state_ref,
    terms_ref,
    total_ref,
    query_ref,
    passage_ref,
    weights,
    state,
    terms,
    raw,
    outs,
    in_sems,
    out_sems,
):
    width = proj_ref.shape[1]
    spread = width // LANES
    rows = (down_ref.shape[0] - EXTRA) // spread
    steps = out_sems.shape[0] // 2
    chunk = proj_ref.shape[0] // steps
    groups = in_sems.shape[0] - 1 - steps
    each = terms_ref.shape[0] // groups
    loads = [pltpu.make_async_copy(state_ref, state, in_sems.at[0])]
    for k in range(groups):
        part = pl.ds(k * each, each)
        loads.append(pltpu.make_async_copy(terms_ref.at[part], terms.at[part], in_sems.at[k + 1]))
    for k in range(steps):
        part = pl.ds(k * chunk, chunk)
        sem = in_sems.at[k + 1 + groups]
        loads.append(pltpu.make_async_copy(proj_ref.at[part], weights.at[part], sem))
    for load in loads:
        load.start()

    def back(k, tiles):
        parts = [tiles[m * rows : (m + 1) * rows] for m in range(spread)]
        incoming = jnp.concatenate(parts, axis=1)
        unit = state[k * rows : (k + 1) * rows, :width]
        inv = state[k * rows : (k + 1) * rows, width : width + 1]
        along = jnp.sum(unit * incoming, axis=-1, keepdims=True)
        raw[k * rows : (k + 1) * rows, :] = (inv * (incoming - unit * along)).astype(bf16)
        return jnp.sum(tiles[spread * rows : spread * rows + 1], axis=1, keepdims=True)

    query = own_ref[0].astype(f32) + other_ref[0].astype(f32)
    query = query + down_ref[...].astype(f32) + up_ref[...].astype(f32)
    loads[0].wait()
    total = back(0, query)
    passage = jnp.zeros(terms_ref.shape[1:], f32)
    for k in range(groups):
        loads[k + 1].wait()
        for n in range(k * each, (k + 1) * each):
            passage = passage + terms[n].astype(f32)
    total = total + back(1, passage)
    total_ref[...] = total * (1.0 / count)
    stores = []
    for k in range(steps):
        part = pl.ds(k * chunk, chunk)
        loads[k + 1 + groups].wait()
        outs[:, part] = lax.dot_general(raw[...], weights[part, :], NT, preferred_element_type=f32)
        for n, out_ref in enumerate((query_ref, passage_ref)):
            source = outs.at[pl.ds(n * rows, rows), part]
            store = pltpu.make_async_copy(source, out_ref.at[:, part], out_sems.at[2 * k + n])
            store.start()
            stores.append(store)
    for store in stores:
        store.wait()


def final(count, own, other, down, up, proj, state, terms):
    rows = state.shape[0] // 2
    depth, width = proj.shape
    steps, groups = 8, 4
    block = pl.BlockSpec((1, *own.shape[1:]), lambda i: (0, 0, 0))
    return pl.pallas_call(
        functools.partial(final_kernel, count),
        grid=(1,),
        in_specs=[block] * 2 + [fixed(down.shape)] * 2 + [HBM] * 3,
        out_specs=[fixed((1, 1)), HBM, HBM],
        out_shape=[sds((1, 1), f32)] + [pltpu.HBM((rows, depth), f32)] * 2,
        scratch_shapes=[
            pltpu.VMEM(proj.shape, bf16),
            pltpu.VMEM(state.shape, f32),
            pltpu.VMEM(terms.shape, bf16),
            pltpu.VMEM((2 * rows, width), bf16),
            pltpu.VMEM((2 * rows, depth), f32),
            pltpu.SemaphoreType.DMA((1 + groups + steps,)),
            pltpu.SemaphoreType.DMA((2 * steps,)),
        ],
        compiler_params=params,
        name="final",
    )(own, other, down, up, *map(in_hbm, (proj, state, terms)))


def gather_queries(message):
    pieces = {0: message}
    down = up = message
    for k in range(1, NZ // 2 + 1):
        down = shift(down, "z", NZ, -1)
        pieces[k] = down
        if k < NZ // 2:
            up = shift(up, "z", NZ, 1)
            pieces[NZ - k] = up
    own = [pieces[k] for k in range(NZ)]
    return own + [swap(piece, "c", NC, 1) for piece in own]


def body(query_pool, passage_pool, proj, positive):
    message, copies, state = embed(query_pool, passage_pool, proj, positive[None])
    passage_tile = lax.all_to_all(copies, QR, 0, 0, tiled=True)
    pieces = gather_queries(message)
    shifted, query_tile, row_sum, column_sum = tile_logits(pieces, passage_tile)
    for pc_step, qr_step in zip(pc_steps, qr_steps):
        row_sum = row_sum + swap(row_sum, *pc_step)
        column_sum = column_sum + swap(column_sum, *qr_step)
    partial, own, other = tile_grads(shifted, row_sum, column_sum, query_tile, passage_tile)
    terms = lax.all_to_all(partial, QR, 0, 0, tiled=True)
    other = swap(other, "c", NC, 1)
    (down,) = ring_step(own, other, [(4, None)])
    came = shift(down, "z", NZ, -1)
    down, up = ring_step(own, other, [(5, came), (3, None)])
    for k in (2, 1):
        came = shift(down, "z", NZ, -1), shift(up, "z", NZ, 1)
        down, up = ring_step(own, other, [(NZ - k, came[0]), (k, came[1])])
    down, up = shift(down, "z", NZ, -1), shift(up, "z", NZ, 1)
    count = 2.0 * column_sum.shape[1] * NZ * NC
    total, grad_query_pool, grad_passage_pool = final(
        count, own, other, down, up, proj, state, terms
    )
    return (total.reshape(()), grad_query_pool, grad_passage_pool)


def solution(mesh):
    fine = Mesh(mesh.devices.reshape(NY, NX, NZ, NC), ("y", "x", "z", "c"))
    in_specs = (
        P(("y", "x", "z", "c"), None),
        P(("z", "c", "y", "x"), None),
        P(),
        P(("y", "x", "z", "c")),
    )
    out_specs = (P(), P(("y", "x", "z", "c"), None), P(("z", "c", "y", "x"), None))
    return jax.shard_map(
        body, mesh=fine, in_specs=in_specs, out_specs=out_specs, check_vma=False
    )
```

```python
import functools

import jax
import jax.numpy as jnp
from jax import lax
from jax.experimental import pallas as pl
from jax.experimental.pallas import tpu as pltpu
from jax.sharding import Mesh, PartitionSpec as P

logit_scale = 20.0
grad_scale = 128.0
norm_eps = 1e-06
log2_e = 1.4426950408889634

NY, NX, NZ, NC = 4, 4, 8, 2
QR = ("y", "x")
PC = ("z", "c")
f32 = jnp.float32
bf16 = jnp.bfloat16
LANES = 128
EXTRA = 16
HBM = pl.BlockSpec(memory_space=pltpu.HBM)
VMEM = pl.BlockSpec(memory_space=pltpu.VMEM)
params = pltpu.CompilerParams(vmem_limit_bytes=24 * 1024 * 1024)
NT = (((1,), (1,)), ((), ()))
TN = (((0,), (0,)), ((), ()))


def shift(value, axis, size, step):
    return lax.ppermute(value, axis, [(i, (i + step) % size) for i in range(size)])


def swap(value, axis, size, bit):
    return lax.ppermute(value, axis, [(i, i ^ bit) for i in range(size)])


def sds(shape, dtype):
    return jax.ShapeDtypeStruct(shape, dtype)


def in_hbm(value):
    return pltpu.with_memory_space_constraint(value, pltpu.HBM)


def in_vmem(value):
    return pltpu.with_memory_space_constraint(value, pltpu.VMEM)


def fixed(shape):
    return pl.BlockSpec(shape, lambda *i: (0,) * len(shape))


def embed_kernel(
    query_ref,
    passage_ref,
    proj_ref,
    positive_ref,
    message_ref,
    copies_ref,
    state_ref,
    weights,
    pools,
    indices,
    spread,
    state,
    in_sems,
    out_sems,
):
    rows, depth = query_ref.shape
    width = proj_ref.shape[1]
    steps = in_sems.shape[0] - 3
    chunk = depth // steps
    loads = [
        pltpu.make_async_copy(query_ref, pools.at[:rows], in_sems.at[0]),
        pltpu.make_async_copy(passage_ref, pools.at[rows:], in_sems.at[1]),
    ]
    for k in range(steps):
        part = pl.ds(k * chunk, chunk)
        loads.append(pltpu.make_async_copy(proj_ref.at[part], weights.at[part], in_sems.at[k + 2]))
    loads.append(pltpu.make_async_copy(positive_ref, indices, in_sems.at[steps + 2]))
    for load in loads:
        load.start()
    loads[0].wait()
    loads[1].wait()
    raw = jnp.zeros((2 * rows, width), f32)
    for k in range(steps):
        loads[k + 2].wait()
        part = pl.ds(k * chunk, chunk)
        raw = raw + jnp.dot(pools[:, part], weights[part, :], preferred_element_type=f32)
    inv = lax.rsqrt(jnp.sum(raw * raw, axis=-1, keepdims=True) + norm_eps)
    unit = raw * inv
    embed = unit.astype(bf16)
    spread[...] = embed[rows:]
    stores = []
    for k in range(copies_ref.shape[0] // rows):
        part = pl.ds(k * rows, rows)
        stores.append(pltpu.make_async_copy(spread, copies_ref.at[part], out_sems.at[k]))
    for store in stores:
        store.start()
    state[:, :width] = unit
    state[:, width:] = jnp.broadcast_to(inv, (2 * rows, LANES))
    stores.append(pltpu.make_async_copy(state, state_ref, out_sems.at[len(stores)]))
    stores[-1].start()
    message_ref[:, :width] = embed[:rows]
    loads[-1].wait()
    square = (rows, rows)
    line = jnp.broadcast_to(indices[...].astype(f32), square)
    on = lax.broadcasted_iota(jnp.int32, square, 0) == lax.broadcasted_iota(jnp.int32, square, 1)
    index = jnp.sum(jnp.where(on, line, 0.0), axis=1, keepdims=True)
    high = jnp.floor(index * (1.0 / LANES))
    low = index - high * LANES
    lane = lax.broadcasted_iota(jnp.int32, (rows, LANES), 1)
    message_ref[:, width:] = jnp.where(lane == 0, high, jnp.where(lane == 1, low, 0.0)).astype(bf16)
    for store in stores:
        store.wait()


def embed(query_pool, passage_pool, proj, positive):
    rows, depth = query_pool.shape
    width = proj.shape[1]
    copies = NY * NX
    steps = 8
    return pl.pallas_call(
        embed_kernel,
        in_specs=[HBM] * 4,
        out_specs=[VMEM, HBM, HBM],
        out_shape=[
            sds((rows, width + LANES), bf16),
            pltpu.HBM((copies * rows, width), bf16),
            pltpu.HBM((2 * rows, width + LANES), f32),
        ],
        scratch_shapes=[
            pltpu.VMEM((depth, width), bf16),
            pltpu.VMEM((2 * rows, depth), bf16),
            pltpu.VMEM((1, rows), jnp.int32),
            pltpu.VMEM((rows, width), bf16),
            pltpu.VMEM((2 * rows, width + LANES), f32),
            pltpu.SemaphoreType.DMA((steps + 3,)),
            pltpu.SemaphoreType.DMA((copies + 1,)),
        ],
        compiler_params=params,
        name="embed",
    )(*map(in_hbm, (query_pool, passage_pool, proj, positive)))


def positive_column(query_ref, part, width, columns):
    words = query_ref[part, width:].astype(f32)
    index = words[:, 0:1] * LANES + words[:, 1:2]
    first = (lax.axis_index("z") * NC + lax.axis_index("c")) * columns
    return index.astype(jnp.int32) - first


def line_of(k):
    z = lax.rem(lax.axis_index("z") + k % NZ, NZ)
    c = lax.axis_index("c")
    return pl.ds((c if k < NZ else 1 - c) * NZ + z, 1)


def logits_kernel(*refs):
    pieces = refs[: NZ * NC]
    passage_ref, exp_ref, query_ref, row_ref, col_ref, row_acc, in_sems = refs[NZ * NC :]
    own = pieces[0].shape[0]
    columns, width = passage_ref.shape
    rows = query_ref.shape[0]
    loads = []
    for k, piece in enumerate(pieces):
        loads.append(pltpu.make_async_copy(piece, query_ref.at[pl.ds(k * own, own)], in_sems.at[k]))
        loads[-1].start()
    steps = 2
    each = rows // steps
    picked = jnp.zeros((1, columns), f32)
    col_sum = jnp.zeros((1, columns), f32)
    for k in range(steps):
        for load in loads[k * each // own : (k + 1) * each // own]:
            load.wait()
        part = pl.ds(k * each, each)
        positive = positive_column(query_ref, part, width, columns)
        dots = lax.dot_general(
            query_ref[part, :width], passage_ref[...], NT, preferred_element_type=f32
        )
        shifted = jnp.exp2(dots * (logit_scale * log2_e) - logit_scale * log2_e)
        exp_ref[part, :] = shifted
        col_sum = col_sum + jnp.sum(shifted, axis=0, keepdims=True)
        row_part = shifted[:, :LANES]
        for n in range(1, columns // LANES):
            row_part = row_part + shifted[:, n * LANES : (n + 1) * LANES]
        row_acc[part, :] = row_part
        column = lax.broadcasted_iota(jnp.int32, (each, columns), 1)
        found = jnp.where(column == positive, dots, 0.0)
        picked = picked + jnp.sum(found, axis=0, keepdims=True)
    col_ref[...] = col_sum
    total = logit_scale * jnp.sum(picked, axis=1, keepdims=True)
    lane = lax.broadcasted_iota(jnp.int32, (1, LANES), 1)
    for k in range(0, NZ * NC, 2):
        turned = row_acc[k * own : (k + 2) * own, :].T
        line = jnp.sum(turned, axis=0, keepdims=True)
        row_ref[line_of(k), :] = jnp.where(lane < own, line, total)
        line = pltpu.roll(line, own, 1)
        row_ref[line_of(k + 1), :] = jnp.where(lane < own, line, total)


def tile_logits(pieces, passage_tile):
    own, wide = pieces[0].shape
    columns, width = passage_tile.shape
    rows = own * len(pieces)
    return pl.pallas_call(
        logits_kernel,
        in_specs=[HBM] * len(pieces) + [VMEM],
        out_specs=[VMEM] * 4,
        out_shape=[
            pltpu.VMEM((rows, columns), f32),
            pltpu.VMEM((rows, wide), bf16),
            sds((len(pieces), LANES), f32),
            sds((1, columns), f32),
        ],
        scratch_shapes=[
            pltpu.VMEM((rows, LANES), f32),
            pltpu.SemaphoreType.DMA((len(pieces),)),
        ],
        compiler_params=params,
        name="logits",
    )(*map(in_hbm, pieces), in_vmem(passage_tile))


def in_thirds(value, shape):
    high = value.astype(bf16).astype(f32)
    middle = (value - high).astype(bf16).astype(f32)
    low = value - high - middle
    lane = lax.broadcasted_iota(jnp.int32, shape, 1)
    parts = jnp.where(lane == 1, middle, jnp.where(lane == 2, low, 0.0))
    return jnp.where(lane == 0, high, parts).astype(bf16)


def as_tiles(out_ref, block, extra):
    rows, width = block.shape
    for m in range(width // LANES):
        out_ref[m * rows : (m + 1) * rows, :] = block[:, m * LANES : (m + 1) * LANES]
    out_ref[width // LANES * rows :, :] = extra


def grads_kernel(
    exp_ref,
    row_ref,
    col_ref,
    query_ref,
    passage_ref,
    part_ref,
    own_ref,
    other_ref,
    grad,
    row_scale,
    query_parts,
    parts,
    sems,
):
    columns, width = passage_ref.shape
    rows = query_ref.shape[0]
    own = rows // (NZ * NC)
    half = 0.5 * grad_scale
    lane = lax.broadcasted_iota(jnp.int32, (1, LANES), 1)
    row_total = logit_scale * rows - 2.0 * row_ref[0:1, own : own + 1]
    for k in range(0, NZ * NC, 2):
        first, second = row_ref[line_of(k), :], row_ref[line_of(k + 1), :]
        line = jnp.where(lane < own, first, pltpu.roll(second, own, 1))
        row_total = row_total + jnp.sum(jnp.log(line), axis=1, keepdims=True)
        turned = jnp.broadcast_to(half / line, (LANES, LANES)).T
        row_scale[k * own : (k + 2) * own, :] = turned
    col_total = jnp.sum(jnp.log(col_ref[...]), axis=1, keepdims=True) + logit_scale * columns
    row_extra = in_thirds(jnp.broadcast_to(row_total, (EXTRA, 1)), (EXTRA, LANES))
    col_extra = in_thirds(jnp.broadcast_to(col_total, (EXTRA, 1)), (EXTRA, LANES))
    stores = []

    def send(blocks, first, count, out_ref, at):
        source, target = blocks.at[pl.ds(first, count)], out_ref.at[pl.ds(at, count)]
        stores.append(pltpu.make_async_copy(source, target, sems.at[len(stores)]))
        stores[-1].start()

    each = rows // 2
    for k in (1, 0):
        part = pl.ds(k * each, each)
        positive = positive_column(query_ref, part, width, columns)
        scale = jnp.concatenate([row_scale[part, :]] * (columns // LANES), axis=1)
        column = lax.broadcasted_iota(jnp.int32, (each, columns), 1)
        hit = jnp.where(column == positive, grad_scale, 0.0)
        tile = (exp_ref[part, :] * (scale + half / col_ref[...]) - hit).astype(bf16)
        grad[part, :] = tile
        term = jnp.dot(tile, passage_ref[...], preferred_element_type=f32)
        term = (logit_scale * term).astype(bf16)
        for n in range(NZ):
            as_tiles(query_parts.at[k * NZ + n], term[n * own : (n + 1) * own, :], col_extra)
        send(query_parts, k * NZ, NZ, other_ref if k else own_ref, 0)
    steps = 4
    chunk = columns // steps
    count = chunk // own
    for k in range(steps):
        part = pl.ds(k * chunk, chunk)
        term = lax.dot_general(
            grad[:, part], query_ref[:, :width], TN, preferred_element_type=f32
        )
        term = (logit_scale * term).astype(bf16)
        for n in range(count):
            as_tiles(parts.at[k * count + n], term[n * own : (n + 1) * own, :], row_extra)
        send(parts, k * count, count, part_ref, k * count)
    for store in stores:
        store.wait()


def tile_grads(shifted, row_sum, column_sum, query_tile, passage_tile):
    rows, wide = query_tile.shape
    columns, width = passage_tile.shape
    own = rows // (NZ * NC)
    block = (own * width // LANES + EXTRA, LANES)
    return pl.pallas_call(
        grads_kernel,
        in_specs=[VMEM] * 5,
        out_specs=[HBM] * 3,
        out_shape=[
            pltpu.HBM((columns // own, *block), bf16),
            pltpu.HBM((NZ, *block), bf16),
            pltpu.HBM((NZ, *block), bf16),
        ],
        scratch_shapes=[
            pltpu.VMEM((rows, columns), bf16),
            pltpu.VMEM((rows, LANES), f32),
            pltpu.VMEM((NZ * NC, *block), bf16),
            pltpu.VMEM((columns // own, *block), bf16),
            pltpu.SemaphoreType.DMA((6,)),
        ],
        compiler_params=params,
        name="grads",
    )(in_vmem(shifted), row_sum, column_sum, in_vmem(query_tile), in_vmem(passage_tile))


def ring_step(own, other, turns):
    _, height, width = own.shape
    operands, in_specs, kept = [], [], []
    for block, came in turns:
        spec = pl.BlockSpec((1, height, width), lambda i, block=block: (block, 0, 0))
        operands += [own, other]
        in_specs += [spec, spec]
        kept.append(came is not None)
        if came is not None:
            operands.append(came)
            in_specs.append(fixed((height, width)))

    def kernel(*refs):
        refs = list(refs)
        outs = refs[len(operands) :]
        for out, there in zip(outs, kept):
            total = refs.pop(0)[0].astype(f32) + refs.pop(0)[0].astype(f32)
            if there:
                total = total + refs.pop(0)[...].astype(f32)
            out[: height - EXTRA, :] = total[: height - EXTRA].astype(bf16)
            extra = jnp.sum(total[height - EXTRA :], axis=1, keepdims=True)
            out[height - EXTRA :, :] = in_thirds(extra, (EXTRA, LANES))

    count = len(turns)
    return pl.pallas_call(
        kernel,
        grid=(1,),
        in_specs=in_specs,
        out_specs=[fixed((height, width))] * count,
        out_shape=[sds((height, width), bf16)] * count,
        compiler_params=params,
        cost_estimate=pl.CostEstimate(flops=1, bytes_accessed=1, transcendentals=0),
        name="ring",
    )(*operands)


def final_kernel(
    count,
    own_ref,
    other_ref,
    down_ref,
    up_ref,
    across_ref,
    proj_ref,
    state_ref,
    terms_ref,
    total_ref,
    query_ref,
    passage_ref,
    weights,
    state,
    terms,
    raw,
    outs,
    in_sems,
    out_sems,
):
    width = proj_ref.shape[1]
    spread = width // LANES
    rows = (down_ref.shape[0] - EXTRA) // spread
    steps = out_sems.shape[0] // 2
    chunk = proj_ref.shape[0] // steps
    groups = in_sems.shape[0] - 1 - steps
    each = terms_ref.shape[0] // groups
    loads = [pltpu.make_async_copy(state_ref, state, in_sems.at[0])]
    for k in range(groups):
        part = pl.ds(k * each, each)
        loads.append(pltpu.make_async_copy(terms_ref.at[part], terms.at[part], in_sems.at[k + 1]))
    for k in range(steps):
        part = pl.ds(k * chunk, chunk)
        sem = in_sems.at[k + 1 + groups]
        loads.append(pltpu.make_async_copy(proj_ref.at[part], weights.at[part], sem))
    for load in loads:
        load.start()

    def back(k, tiles):
        parts = [tiles[m * rows : (m + 1) * rows] for m in range(spread)]
        incoming = jnp.concatenate(parts, axis=1)
        unit = state[k * rows : (k + 1) * rows, :width]
        inv = state[k * rows : (k + 1) * rows, width : width + 1]
        along = jnp.sum(unit * incoming, axis=-1, keepdims=True)
        raw[k * rows : (k + 1) * rows, :] = (inv * (incoming - unit * along)).astype(bf16)
        return jnp.sum(tiles[spread * rows : spread * rows + 1], axis=1, keepdims=True)

    query = own_ref[0].astype(f32) + other_ref[0].astype(f32)
    for ref in (down_ref, up_ref, across_ref):
        query = query + ref[...].astype(f32)
    loads[0].wait()
    total = back(0, query)
    passage = jnp.zeros(terms_ref.shape[1:], f32)
    for k in range(groups):
        loads[k + 1].wait()
        for n in range(k * each, (k + 1) * each):
            passage = passage + terms[n].astype(f32)
    total = total + back(1, passage)
    total_ref[...] = total * (1.0 / count)
    stores = []
    for k in range(steps):
        part = pl.ds(k * chunk, chunk)
        loads[k + 1 + groups].wait()
        outs[:, part] = lax.dot_general(raw[...], weights[part, :], NT, preferred_element_type=f32)
        for n, out_ref in enumerate((query_ref, passage_ref)):
            source = outs.at[pl.ds(n * rows, rows), part]
            store = pltpu.make_async_copy(source, out_ref.at[:, part], out_sems.at[2 * k + n])
            store.start()
            stores.append(store)
    for store in stores:
        store.wait()


def final(count, own, other, down, up, across, proj, state, terms):
    rows = state.shape[0] // 2
    depth, width = proj.shape
    steps, groups = 8, 4
    block = pl.BlockSpec((1, *own.shape[1:]), lambda i: (0, 0, 0))
    return pl.pallas_call(
        functools.partial(final_kernel, count),
        grid=(1,),
        in_specs=[block] * 2 + [fixed(down.shape)] * 3 + [HBM] * 3,
        out_specs=[fixed((1, 1)), HBM, HBM],
        out_shape=[sds((1, 1), f32)] + [pltpu.HBM((rows, depth), f32)] * 2,
        scratch_shapes=[
            pltpu.VMEM(proj.shape, bf16),
            pltpu.VMEM(state.shape, f32),
            pltpu.VMEM(terms.shape, bf16),
            pltpu.VMEM((2 * rows, width), bf16),
            pltpu.VMEM((2 * rows, depth), f32),
            pltpu.SemaphoreType.DMA((1 + groups + steps,)),
            pltpu.SemaphoreType.DMA((2 * steps,)),
        ],
        compiler_params=params,
        name="final",
    )(own, other, down, up, across, *map(in_hbm, (proj, state, terms)))


def gather_queries(message):
    pieces = {0: message}
    down = up = message
    for k in range(1, NZ // 2 + 1):
        down = shift(down, "z", NZ, -1)
        pieces[k] = down
        if k < NZ // 2:
            up = shift(up, "z", NZ, 1)
            pieces[NZ - k] = up
    own = [pieces[k] for k in range(NZ)]
    return own + [swap(piece, "c", NC, 1) for piece in own]


def body(query_pool, passage_pool, proj, positive):
    message, copies, state = embed(query_pool, passage_pool, proj, positive[None])
    passage_tile = lax.all_to_all(copies, QR, 0, 0, tiled=True)
    pieces = gather_queries(message)
    shifted, query_tile, row_sum, column_sum = tile_logits(pieces, passage_tile)
    row_sum = row_sum + swap(row_sum, "c", NC, 1)
    column_sum = column_sum + sum(shift(column_sum, "x", NX, k) for k in range(1, NX))
    before, after = shift(row_sum, "z", NZ, 1), shift(row_sum, "z", NZ, -1)
    column_sum = column_sum + sum(shift(column_sum, "y", NY, k) for k in range(1, NY))
    pair = row_sum + before
    three = pair + after
    row_sum = three + shift(three, "z", NZ, -3) + shift(pair, "z", NZ, 2)
    partial, own, other = tile_grads(shifted, row_sum, column_sum, query_tile, passage_tile)
    terms = lax.all_to_all(partial, QR, 0, 0, tiled=True)
    other = swap(other, "c", NC, 1)
    far = NZ // 2
    down, up, across = ring_step(own, other, [(far + 1, None), (far - 1, None), (far, None)])
    across = shift(across, "z", NZ, far)
    for k in range(far - 2, 0, -1):
        came = shift(down, "z", NZ, -1), shift(up, "z", NZ, 1)
        down, up = ring_step(own, other, [(NZ - k, came[0]), (k, came[1])])
    down, up = shift(down, "z", NZ, -1), shift(up, "z", NZ, 1)
    count = 2.0 * column_sum.shape[1] * NZ * NC
    total, grad_query_pool, grad_passage_pool = final(
        count, own, other, down, up, across, proj, state, terms
    )
    return (total.reshape(()), grad_query_pool, grad_passage_pool)


def solution(mesh):
    fine = Mesh(mesh.devices.reshape(NY, NX, NZ, NC), ("y", "x", "z", "c"))
    in_specs = (
        P(("y", "x", "z", "c"), None),
        P(("z", "c", "y", "x"), None),
        P(),
        P(("y", "x", "z", "c")),
    )
    out_specs = (P(), P(("y", "x", "z", "c"), None), P(("z", "c", "y", "x"), None))
    return jax.shard_map(
        body, mesh=fine, in_specs=in_specs, out_specs=out_specs, check_vma=False
    )
```

```python
import functools

import jax
import jax.numpy as jnp
from jax import lax
from jax.experimental import pallas as pl
from jax.experimental.pallas import tpu as pltpu
from jax.sharding import Mesh, PartitionSpec as P

logit_scale = 20.0
grad_scale = 128.0
norm_eps = 1e-06
log2_e = 1.4426950408889634

NY, NX, NZ, NC = 4, 4, 8, 2
QR = ("y", "x")
PC = ("z", "c")
f32 = jnp.float32
bf16 = jnp.bfloat16
LANES = 128
EXTRA = 16
HBM = pl.BlockSpec(memory_space=pltpu.HBM)
VMEM = pl.BlockSpec(memory_space=pltpu.VMEM)
params = pltpu.CompilerParams(vmem_limit_bytes=24 * 1024 * 1024)
NT = (((1,), (1,)), ((), ()))
TN = (((0,), (0,)), ((), ()))


def shift(value, axis, size, step):
    return lax.ppermute(value, axis, [(i, (i + step) % size) for i in range(size)])


def swap(value, axis, size, bit):
    return lax.ppermute(value, axis, [(i, i ^ bit) for i in range(size)])


def sds(shape, dtype):
    return jax.ShapeDtypeStruct(shape, dtype)


def in_hbm(value):
    return pltpu.with_memory_space_constraint(value, pltpu.HBM)


def in_vmem(value):
    return pltpu.with_memory_space_constraint(value, pltpu.VMEM)


def fixed(shape):
    return pl.BlockSpec(shape, lambda *i: (0,) * len(shape))


def embed_kernel(
    query_ref,
    passage_ref,
    proj_ref,
    positive_ref,
    message_ref,
    copies_ref,
    state_ref,
    weights,
    pools,
    indices,
    spread,
    state,
    in_sems,
    out_sems,
):
    rows, depth = query_ref.shape
    width = proj_ref.shape[1]
    steps = in_sems.shape[0] - 3
    chunk = depth // steps
    loads = [
        pltpu.make_async_copy(query_ref, pools.at[:rows], in_sems.at[0]),
        pltpu.make_async_copy(passage_ref, pools.at[rows:], in_sems.at[1]),
    ]
    for k in range(steps):
        part = pl.ds(k * chunk, chunk)
        loads.append(pltpu.make_async_copy(proj_ref.at[part], weights.at[part], in_sems.at[k + 2]))
    loads.append(pltpu.make_async_copy(positive_ref, indices, in_sems.at[steps + 2]))
    for load in loads:
        load.start()
    loads[0].wait()
    loads[1].wait()
    raw = jnp.zeros((2 * rows, width), f32)
    for k in range(steps):
        loads[k + 2].wait()
        part = pl.ds(k * chunk, chunk)
        raw = raw + jnp.dot(pools[:, part], weights[part, :], preferred_element_type=f32)
    inv = lax.rsqrt(jnp.sum(raw * raw, axis=-1, keepdims=True) + norm_eps)
    unit = raw * inv
    embed = unit.astype(bf16)
    spread[...] = embed[rows:]
    stores = []
    for k in range(copies_ref.shape[0] // rows):
        part = pl.ds(k * rows, rows)
        stores.append(pltpu.make_async_copy(spread, copies_ref.at[part], out_sems.at[k]))
    for store in stores:
        store.start()
    state[:, :width] = unit
    state[:, width:] = jnp.broadcast_to(inv, (2 * rows, LANES))
    stores.append(pltpu.make_async_copy(state, state_ref, out_sems.at[len(stores)]))
    stores[-1].start()
    message_ref[:, :width] = embed[:rows]
    loads[-1].wait()
    square = (rows, rows)
    line = jnp.broadcast_to(indices[...].astype(f32), square)
    on = lax.broadcasted_iota(jnp.int32, square, 0) == lax.broadcasted_iota(jnp.int32, square, 1)
    index = jnp.sum(jnp.where(on, line, 0.0), axis=1, keepdims=True)
    high = jnp.floor(index * (1.0 / LANES))
    low = index - high * LANES
    lane = lax.broadcasted_iota(jnp.int32, (rows, LANES), 1)
    message_ref[:, width:] = jnp.where(lane == 0, high, jnp.where(lane == 1, low, 0.0)).astype(bf16)
    for store in stores:
        store.wait()


def embed(query_pool, passage_pool, proj, positive):
    rows, depth = query_pool.shape
    width = proj.shape[1]
    copies = NY * NX
    steps = 8
    return pl.pallas_call(
        embed_kernel,
        in_specs=[HBM] * 4,
        out_specs=[VMEM, HBM, HBM],
        out_shape=[
            sds((rows, width + LANES), bf16),
            pltpu.HBM((copies * rows, width), bf16),
            pltpu.HBM((2 * rows, width + LANES), f32),
        ],
        scratch_shapes=[
            pltpu.VMEM((depth, width), bf16),
            pltpu.VMEM((2 * rows, depth), bf16),
            pltpu.VMEM((1, rows), jnp.int32),
            pltpu.VMEM((rows, width), bf16),
            pltpu.VMEM((2 * rows, width + LANES), f32),
            pltpu.SemaphoreType.DMA((steps + 3,)),
            pltpu.SemaphoreType.DMA((copies + 1,)),
        ],
        compiler_params=params,
        name="embed",
    )(*map(in_hbm, (query_pool, passage_pool, proj, positive)))


def positive_column(query_ref, part, width, columns):
    words = query_ref[part, width:].astype(f32)
    index = words[:, 0:1] * LANES + words[:, 1:2]
    first = (lax.axis_index("z") * NC + lax.axis_index("c")) * columns
    return index.astype(jnp.int32) - first


def line_of(k):
    z = lax.rem(lax.axis_index("z") + k % NZ, NZ)
    c = lax.axis_index("c")
    return pl.ds((c if k < NZ else 1 - c) * NZ + z, 1)


def logits_kernel(*refs):
    pieces = refs[: NZ * NC]
    passage_ref, exp_ref, query_ref, row_ref, col_ref, row_acc, in_sems = refs[NZ * NC :]
    own = pieces[0].shape[0]
    columns, width = passage_ref.shape
    rows = query_ref.shape[0]
    loads = []
    for k, piece in enumerate(pieces):
        loads.append(pltpu.make_async_copy(piece, query_ref.at[pl.ds(k * own, own)], in_sems.at[k]))
        loads[-1].start()
    steps = 2
    each = rows // steps
    picked = jnp.zeros((1, columns), f32)
    col_sum = jnp.zeros((1, columns), f32)
    for k in range(steps):
        for load in loads[k * each // own : (k + 1) * each // own]:
            load.wait()
        part = pl.ds(k * each, each)
        positive = positive_column(query_ref, part, width, columns)
        dots = lax.dot_general(
            query_ref[part, :width], passage_ref[...], NT, preferred_element_type=f32
        )
        shifted = jnp.exp2(dots * (logit_scale * log2_e) - logit_scale * log2_e)
        exp_ref[part, :] = shifted
        col_sum = col_sum + jnp.sum(shifted, axis=0, keepdims=True)
        row_part = shifted[:, :LANES]
        for n in range(1, columns // LANES):
            row_part = row_part + shifted[:, n * LANES : (n + 1) * LANES]
        row_acc[part, :] = row_part
        column = lax.broadcasted_iota(jnp.int32, (each, columns), 1)
        found = jnp.where(column == positive, dots, 0.0)
        picked = picked + jnp.sum(found, axis=0, keepdims=True)
    col_ref[...] = col_sum
    total = logit_scale * jnp.sum(picked, axis=1, keepdims=True)
    lane = lax.broadcasted_iota(jnp.int32, (1, LANES), 1)
    for k in range(0, NZ * NC, 2):
        turned = row_acc[k * own : (k + 2) * own, :].T
        line = jnp.sum(turned, axis=0, keepdims=True)
        row_ref[line_of(k), :] = jnp.where(lane < own, line, total)
        line = pltpu.roll(line, own, 1)
        row_ref[line_of(k + 1), :] = jnp.where(lane < own, line, total)


def tile_logits(pieces, passage_tile):
    own, wide = pieces[0].shape
    columns, width = passage_tile.shape
    rows = own * len(pieces)
    return pl.pallas_call(
        logits_kernel,
        in_specs=[HBM] * len(pieces) + [VMEM],
        out_specs=[VMEM] * 4,
        out_shape=[
            pltpu.VMEM((rows, columns), f32),
            pltpu.VMEM((rows, wide), bf16),
            sds((len(pieces), LANES), f32),
            sds((1, columns), f32),
        ],
        scratch_shapes=[
            pltpu.VMEM((rows, LANES), f32),
            pltpu.SemaphoreType.DMA((len(pieces),)),
        ],
        compiler_params=params,
        name="logits",
    )(*map(in_hbm, pieces), in_vmem(passage_tile))


def in_thirds(value, shape):
    high = value.astype(bf16).astype(f32)
    middle = (value - high).astype(bf16).astype(f32)
    low = value - high - middle
    lane = lax.broadcasted_iota(jnp.int32, shape, 1)
    parts = jnp.where(lane == 1, middle, jnp.where(lane == 2, low, 0.0))
    return jnp.where(lane == 0, high, parts).astype(bf16)


def as_tiles(out_ref, block, extra):
    rows, width = block.shape
    for m in range(width // LANES):
        out_ref[m * rows : (m + 1) * rows, :] = block[:, m * LANES : (m + 1) * LANES]
    out_ref[width // LANES * rows :, :] = extra


def grads_kernel(
    exp_ref,
    row_ref,
    col_ref,
    query_ref,
    passage_ref,
    part_ref,
    own_ref,
    other_ref,
    grad,
    row_scale,
    query_parts,
    parts,
    sems,
):
    columns, width = passage_ref.shape
    rows = query_ref.shape[0]
    own = rows // (NZ * NC)
    half = 0.5 * grad_scale
    lane = lax.broadcasted_iota(jnp.int32, (1, LANES), 1)
    row_total = logit_scale * rows - 2.0 * row_ref[0:1, own : own + 1]
    for k in range(0, NZ * NC, 2):
        first, second = row_ref[line_of(k), :], row_ref[line_of(k + 1), :]
        line = jnp.where(lane < own, first, pltpu.roll(second, own, 1))
        row_total = row_total + jnp.sum(jnp.log(line), axis=1, keepdims=True)
        turned = jnp.broadcast_to(half / line, (LANES, LANES)).T
        row_scale[k * own : (k + 2) * own, :] = turned
    col_total = jnp.sum(jnp.log(col_ref[...]), axis=1, keepdims=True) + logit_scale * columns
    row_extra = in_thirds(jnp.broadcast_to(row_total, (EXTRA, 1)), (EXTRA, LANES))
    col_extra = in_thirds(jnp.broadcast_to(col_total, (EXTRA, 1)), (EXTRA, LANES))
    stores = []

    def send(blocks, first, count, out_ref, at):
        source, target = blocks.at[pl.ds(first, count)], out_ref.at[pl.ds(at, count)]
        stores.append(pltpu.make_async_copy(source, target, sems.at[len(stores)]))
        stores[-1].start()

    each = rows // 2
    for k in (1, 0):
        part = pl.ds(k * each, each)
        positive = positive_column(query_ref, part, width, columns)
        scale = jnp.concatenate([row_scale[part, :]] * (columns // LANES), axis=1)
        column = lax.broadcasted_iota(jnp.int32, (each, columns), 1)
        hit = jnp.where(column == positive, grad_scale, 0.0)
        tile = (exp_ref[part, :] * (scale + half / col_ref[...]) - hit).astype(bf16)
        grad[part, :] = tile
        term = jnp.dot(tile, passage_ref[...], preferred_element_type=f32)
        term = (logit_scale * term).astype(bf16)
        for n in range(NZ):
            as_tiles(query_parts.at[k * NZ + n], term[n * own : (n + 1) * own, :], col_extra)
        send(query_parts, k * NZ, NZ, other_ref if k else own_ref, 0)
    steps = 4
    chunk = columns // steps
    count = chunk // own
    for k in range(steps):
        part = pl.ds(k * chunk, chunk)
        term = lax.dot_general(
            grad[:, part], query_ref[:, :width], TN, preferred_element_type=f32
        )
        term = (logit_scale * term).astype(bf16)
        for n in range(count):
            as_tiles(parts.at[k * count + n], term[n * own : (n + 1) * own, :], row_extra)
        send(parts, k * count, count, part_ref, k * count)
    for store in stores:
        store.wait()


def tile_grads(shifted, row_sum, column_sum, query_tile, passage_tile):
    rows, wide = query_tile.shape
    columns, width = passage_tile.shape
    own = rows // (NZ * NC)
    block = (own * width // LANES + EXTRA, LANES)
    return pl.pallas_call(
        grads_kernel,
        in_specs=[VMEM] * 5,
        out_specs=[HBM] * 3,
        out_shape=[
            pltpu.HBM((columns // own, *block), bf16),
            pltpu.HBM((NZ, *block), bf16),
            pltpu.HBM((NZ, *block), bf16),
        ],
        scratch_shapes=[
            pltpu.VMEM((rows, columns), bf16),
            pltpu.VMEM((rows, LANES), f32),
            pltpu.VMEM((NZ * NC, *block), bf16),
            pltpu.VMEM((columns // own, *block), bf16),
            pltpu.SemaphoreType.DMA((6,)),
        ],
        compiler_params=params,
        name="grads",
    )(in_vmem(shifted), row_sum, column_sum, in_vmem(query_tile), in_vmem(passage_tile))


def ring_step(own, other, turns):
    _, height, width = own.shape
    operands, in_specs, kept = [], [], []
    for block, came in turns:
        spec = pl.BlockSpec((1, height, width), lambda i, block=block: (block, 0, 0))
        operands += [own, other]
        in_specs += [spec, spec]
        kept.append(came is not None)
        if came is not None:
            operands.append(came)
            in_specs.append(fixed((height, width)))

    def kernel(*refs):
        refs = list(refs)
        outs = refs[len(operands) :]
        for out, there in zip(outs, kept):
            total = refs.pop(0)[0].astype(f32) + refs.pop(0)[0].astype(f32)
            if there:
                total = total + refs.pop(0)[...].astype(f32)
            out[: height - EXTRA, :] = total[: height - EXTRA].astype(bf16)
            extra = jnp.sum(total[height - EXTRA :], axis=1, keepdims=True)
            out[height - EXTRA :, :] = in_thirds(extra, (EXTRA, LANES))

    count = len(turns)
    return pl.pallas_call(
        kernel,
        grid=(1,),
        in_specs=in_specs,
        out_specs=[fixed((height, width))] * count,
        out_shape=[sds((height, width), bf16)] * count,
        compiler_params=params,
        cost_estimate=pl.CostEstimate(flops=1, bytes_accessed=1, transcendentals=0),
        name="ring",
    )(*operands)


def final_kernel(
    count,
    own_ref,
    other_ref,
    down_ref,
    up_ref,
    across_ref,
    proj_ref,
    state_ref,
    terms_ref,
    total_ref,
    query_ref,
    passage_ref,
    weights,
    state,
    terms,
    raw,
    outs,
    in_sems,
    out_sems,
):
    width = proj_ref.shape[1]
    spread = width // LANES
    rows = (down_ref.shape[0] - EXTRA) // spread
    steps = out_sems.shape[0] // 2
    chunk = proj_ref.shape[0] // steps
    groups = in_sems.shape[0] - 1 - steps
    each = terms_ref.shape[0] // groups
    loads = [pltpu.make_async_copy(state_ref, state, in_sems.at[0])]
    for k in range(groups):
        part = pl.ds(k * each, each)
        loads.append(pltpu.make_async_copy(terms_ref.at[part], terms.at[part], in_sems.at[k + 1]))
    for k in range(steps):
        part = pl.ds(k * chunk, chunk)
        sem = in_sems.at[k + 1 + groups]
        loads.append(pltpu.make_async_copy(proj_ref.at[part], weights.at[part], sem))
    for load in loads:
        load.start()

    def back(k, tiles):
        parts = [tiles[m * rows : (m + 1) * rows] for m in range(spread)]
        incoming = jnp.concatenate(parts, axis=1)
        unit = state[k * rows : (k + 1) * rows, :width]
        inv = state[k * rows : (k + 1) * rows, width : width + 1]
        along = jnp.sum(unit * incoming, axis=-1, keepdims=True)
        raw[k * rows : (k + 1) * rows, :] = (inv * (incoming - unit * along)).astype(bf16)
        return jnp.sum(tiles[spread * rows : spread * rows + 1], axis=1, keepdims=True)

    query = own_ref[0].astype(f32) + other_ref[0].astype(f32)
    for ref in (down_ref, up_ref, across_ref):
        query = query + ref[...].astype(f32)
    loads[0].wait()
    total = back(0, query)
    passage = jnp.zeros(terms_ref.shape[1:], f32)
    for k in range(groups):
        loads[k + 1].wait()
        for n in range(k * each, (k + 1) * each):
            passage = passage + terms[n].astype(f32)
    total = total + back(1, passage)
    total_ref[...] = total * (1.0 / count)
    stores = []
    for k in range(steps):
        part = pl.ds(k * chunk, chunk)
        loads[k + 1 + groups].wait()
        outs[:, part] = lax.dot_general(raw[...], weights[part, :], NT, preferred_element_type=f32)
        for n, out_ref in enumerate((query_ref, passage_ref)):
            source = outs.at[pl.ds(n * rows, rows), part]
            store = pltpu.make_async_copy(source, out_ref.at[:, part], out_sems.at[2 * k + n])
            store.start()
            stores.append(store)
    for store in stores:
        store.wait()


def final(count, own, other, down, up, across, proj, state, terms):
    rows = state.shape[0] // 2
    depth, width = proj.shape
    steps, groups = 8, 4
    block = pl.BlockSpec((1, *own.shape[1:]), lambda i: (0, 0, 0))
    return pl.pallas_call(
        functools.partial(final_kernel, count),
        grid=(1,),
        in_specs=[block] * 2 + [fixed(down.shape)] * 3 + [HBM] * 3,
        out_specs=[fixed((1, 1)), HBM, HBM],
        out_shape=[sds((1, 1), f32)] + [pltpu.HBM((rows, depth), f32)] * 2,
        scratch_shapes=[
            pltpu.VMEM(proj.shape, bf16),
            pltpu.VMEM(state.shape, f32),
            pltpu.VMEM(terms.shape, bf16),
            pltpu.VMEM((2 * rows, width), bf16),
            pltpu.VMEM((2 * rows, depth), f32),
            pltpu.SemaphoreType.DMA((1 + groups + steps,)),
            pltpu.SemaphoreType.DMA((2 * steps,)),
        ],
        compiler_params=params,
        name="final",
    )(own, other, down, up, across, *map(in_hbm, (proj, state, terms)))


def gather_queries(message):
    far = NZ // 2
    pieces = {0: message, far: shift(message, "z", NZ, far)}
    down = up = message
    for k in range(1, far):
        down, up = shift(down, "z", NZ, -1), shift(up, "z", NZ, 1)
        pieces[k], pieces[NZ - k] = down, up
    own = [pieces[k] for k in range(NZ)]
    return own + [swap(piece, "c", NC, 1) for piece in own]


def body(query_pool, passage_pool, proj, positive):
    message, copies, state = embed(query_pool, passage_pool, proj, positive[None])
    passage_tile = lax.all_to_all(copies, QR, 0, 0, tiled=True)
    pieces = gather_queries(message)
    shifted, query_tile, row_sum, column_sum = tile_logits(pieces, passage_tile)
    row_sum = row_sum + swap(row_sum, "c", NC, 1)
    column_sum = column_sum + sum(shift(column_sum, "x", NX, k) for k in range(1, NX))
    before, after = shift(row_sum, "z", NZ, 1), shift(row_sum, "z", NZ, -1)
    column_sum = column_sum + sum(shift(column_sum, "y", NY, k) for k in range(1, NY))
    pair = row_sum + before
    three = pair + after
    row_sum = three + shift(three, "z", NZ, -3) + shift(pair, "z", NZ, 2)
    partial, own, other = tile_grads(shifted, row_sum, column_sum, query_tile, passage_tile)
    terms = lax.all_to_all(partial, QR, 0, 0, tiled=True)
    other = swap(other, "c", NC, 1)
    far = NZ // 2
    down, up, across = ring_step(own, other, [(far + 1, None), (far - 1, None), (far, None)])
    across = shift(across, "z", NZ, far)
    for k in range(far - 2, 0, -1):
        came = shift(down, "z", NZ, -1), shift(up, "z", NZ, 1)
        down, up = ring_step(own, other, [(NZ - k, came[0]), (k, came[1])])
    down, up = shift(down, "z", NZ, -1), shift(up, "z", NZ, 1)
    count = 2.0 * column_sum.shape[1] * NZ * NC
    total, grad_query_pool, grad_passage_pool = final(
        count, own, other, down, up, across, proj, state, terms
    )
    return (total.reshape(()), grad_query_pool, grad_passage_pool)


def solution(mesh):
    fine = Mesh(mesh.devices.reshape(NY, NX, NZ, NC), ("y", "x", "z", "c"))
    in_specs = (
        P(("y", "x", "z", "c"), None),
        P(("z", "c", "y", "x"), None),
        P(),
        P(("y", "x", "z", "c")),
    )
    out_specs = (P(), P(("y", "x", "z", "c"), None), P(("z", "c", "y", "x"), None))
    return jax.shard_map(
        body, mesh=fine, in_specs=in_specs, out_specs=out_specs, check_vma=False
    )
```
